256 devices in a mesh: pair: 4 (over y_lo, core), row: 64 (over y_hi, x, z).
Axes of the slice: x: 4, y: 4 (y_hi: 2, y_lo: 2; y = y_hi * 2 + y_lo), z: 8, core: 2. Of those that a mesh axis runs over, the one named last changes fastest.
Arguments:
- integrals: float32 [128, 1600, 1600], P('pair', 'row'), may hold values from -6 to 6
- coeffs: float32 [1600, 1024], replicated, may hold values from -0.15625 to 0.15625
- pair_list: int32 [128, 2], replicated, may hold values from 0 to 1599, as said below
Outputs:
- transformed: float32 [1024, 64, 1024], P(('pair', 'row'))
The draws below stay inside these ranges and needn't reach their ends.
Inputs may be any that keep to these rules, and one draw needn't show every extreme that they name: `pair_list`: each row is a pair (p, q) of atomic orbital indices with p >= q; some rows have p == q.
All inputs are finite; a program needn't handle non-finite values.
Results may differ from the reference program's by a relative error of at most 0.000071.
Values sent between devices are 32-bit elements; how exact they have to be, the bound alone decides.
A program may use at most 128 MiB of HBM per device.

```python
import jax
import jax.numpy as jnp
from jax import lax

NBF = 1600
NMO = 1024
NACT = 8
PAIRS = 128


def draw_pair_list(key, part):
    key = jax.random.fold_in(key, 11)
    key_first, key_second = jax.random.split(key)
    first = jax.random.randint(key_first, (PAIRS,), 0, NBF)
    second = jax.random.randint(key_second, (PAIRS,), 0, NBF) % (first + 1)
    first = first.at[0].set(NBF - 1)
    second = second.at[0].set(0)
    second = second.at[1].set(first[1])
    return jnp.stack([first, second], axis=1).astype(jnp.int32)


def block_levels(rng, extent, pieces, smallest, high):
    loudness, own = 1.0, jax.random.fold_in(rng, 6)
    for position, parts in pieces:
        heights = jnp.exp(jax.random.uniform(jax.random.fold_in(own, position), (parts,), jnp.float32, smallest / len(pieces), high / len(pieces)))
        loudness = loudness * jnp.repeat(heights, extent[position] // parts).reshape([-1 if axis == position else 1 for axis in range(len(extent))])
    return loudness


def normal_values(stream_key, shape, spread, most, pieces=(), kind=jnp.bfloat16):
    drawn = spread * jax.random.normal(stream_key, shape, jnp.float32)
    if pieces:
        drawn = drawn * block_levels(stream_key, shape, pieces, -0.22, 0.18)
    return jnp.clip(drawn, -most, most).astype(kind)


def setup_inputs(seed: int = 0) -> dict:
    streams_of = jax.random.split(jax.random.key(seed), 4)
    integrals = normal_values(streams_of[0], (PAIRS, NBF, NBF), 1.0, 6.0, ((0, 4), (1, 64)), jnp.float32)
    coeffs = normal_values(streams_of[1], (NBF, NMO), NBF ** -0.5, 0.15625, (), jnp.float32)
    pair_list = draw_pair_list(jax.random.fold_in(streams_of[3], 71), 0)
    return {"integrals": integrals, "coeffs": coeffs, "pair_list": pair_list}


def reference(integrals, coeffs, pair_list):
    high = lax.Precision.HIGHEST
    quarter_s = jnp.einsum('sb,nrs->bnr', coeffs, integrals, precision=high)
    quarter_r = jnp.einsum('bnr,ra->bna', quarter_s, coeffs, precision=high)
    first = coeffs[pair_list[:, 0], :NACT]
    second = coeffs[pair_list[:, 1], :NACT]
    distinct = (pair_list[:, 0] != pair_list[:, 1]).astype(jnp.float32)
    weights = jnp.einsum('ni,nj->ijn', first, second) + distinct[None, None, :] * jnp.einsum('ni,nj->ijn', second, first)
    weights = weights.reshape(NACT * NACT, PAIRS)
    factor = NBF / jnp.sqrt(jnp.float32(2 * PAIRS))
    return factor * jnp.einsum('mn,bna->bma', weights, quarter_r, precision=high)
```

```python
import functools

import jax
import jax.numpy as jnp
from jax import lax
from jax.experimental import pallas as pl
from jax.experimental.pallas import tpu as pltpu
from jax.sharding import PartitionSpec as P

F32, BF16 = jnp.float32, jnp.bfloat16
NACT = 8
STARTS = [8 * i - i * (i - 1) // 2 for i in range(NACT)]
NSYM = 36
GROUP = 40
LANES = 128


def iota(shape, dim):
    return lax.broadcasted_iota(jnp.int32, shape, dim)


def split(x):
    hi = x.astype(BF16)
    return hi, (x - hi.astype(F32)).astype(BF16)


def dot(a, b, ca=1, cb=0, precision=None):
    return lax.dot_general(
        a, b, (((ca,), (cb,)), ((), ())), precision=precision, preferred_element_type=F32
    )


def dot3(a, b, ca=1, cb=0):
    (ah, al), (bh, bl) = a, b
    return dot(ah, bh, ca, cb) + (dot(ah, bl, ca, cb) + dot(al, bh, ca, cb))


def exact(a, b, ca=1, cb=0):
    return dot(a, b, ca, cb, lax.Precision.HIGHEST)


def first_second(m):
    i = jnp.zeros_like(m)
    start = jnp.zeros_like(m)
    for t in range(1, NACT):
        past = (m >= STARTS[t]).astype(jnp.int32)
        i = i + past
        start = start + past * (STARTS[t] - STARTS[t - 1])
    return i, m - start + i


def sym_index(ij):
    i, j = ij >> 3, ij & 7
    low, high = jnp.minimum(i, j), jnp.maximum(i, j)
    return 8 * low - ((low * (low - 1)) >> 1) + high - low


def make_weights(pair, pair_ref, c_ref, slim_ref, rows_ref):
    pairs_dev = rows_ref.shape[0] // 3
    slim_ref[...] = c_ref[:, 0:LANES]

    def pick(n, carry):
        p = pair_ref[pair * pairs_dev + n, 0]
        q = pair_ref[pair * pairs_dev + n, 1]
        rows_ref[pl.ds(n, 1), :] = slim_ref[pl.ds(p, 1), :]
        rows_ref[pl.ds(pairs_dev + n, 1), :] = slim_ref[pl.ds(q, 1), :]
        rows_ref[pl.ds(2 * pairs_dev + n, 1), :] = jnp.full((1, LANES), jnp.where(p != q, 1.0, 0.0), F32)
        return carry

    lax.fori_loop(0, pairs_dev, pick, 0)
    k, m = iota((LANES, LANES), 0), iota((LANES, LANES), 1)
    i, j = first_second(m)
    sel_i = jnp.where((k == i) & (m < NSYM), 1.0, 0.0).astype(F32)
    sel_j = jnp.where((k == j) & (m < NSYM), 1.0, 0.0).astype(F32)
    first, second, distinct = (rows_ref[t * pairs_dev : (t + 1) * pairs_dev, :] for t in range(3))
    weights = exact(first, sel_i) * exact(second, sel_j) + distinct * (
        exact(second, sel_i) * exact(first, sel_j)
    )
    spread = jnp.where(iota((pairs_dev, pairs_dev * 8), 0) == lax.rem(iota((pairs_dev, pairs_dev * 8), 1), pairs_dev), 1.0, 0.0).astype(F32)
    wide = exact(weights, spread, 0, 0)[:GROUP]
    column = lax.div(iota((GROUP, pairs_dev * 8), 1), pairs_dev)
    kron = jnp.concatenate([jnp.where(column == j, wide, 0.0) for j in range(8)], axis=0)
    row, m = iota((64, LANES), 0), iota((64, LANES), 1)
    last = jnp.where(((row & 7) < 5) & (m == 5 * (row >> 3) + (row & 7)), 1.0, 0.0).astype(F32)
    return split(kron), split(exact(last, weights, 1, 1))


def sum_pairs(x_ref, kron, last, vh_ref, vl_ref, s0, width):
    pairs_dev = x_ref.shape[1]
    cols = pl.ds(s0, width)
    parts = [
        dot3(kron, split(x_ref[8 * q : 8 * q + 8, :, cols].reshape(pairs_dev * 8, width))) for q in range(3)
    ]
    tail = dot3(last, split(x_ref[24, :, cols]))
    for j in range(8):
        block = jnp.concatenate(
            [part[GROUP * j : GROUP * (j + 1)] for part in parts] + [tail[8 * j : 8 * j + 8]], axis=0
        )
        hi, lo = split(block)
        vh_ref[LANES * j : LANES * (j + 1), cols] = hi
        vl_ref[LANES * j : LANES * (j + 1), cols] = lo


def sum_all_pairs(x_ref, kron, last, vh_ref, vl_ref):
    basis = x_ref.shape[2]
    step = 256
    whole = basis // step

    def some(t, carry):
        sum_pairs(x_ref, kron, last, vh_ref, vl_ref, pl.multiple_of(t * step, step), step)
        return carry

    lax.fori_loop(0, whole, some, 0)
    if basis % step:
        sum_pairs(x_ref, kron, last, vh_ref, vl_ref, whole * step, basis % step)


def split_coeffs(c_ref, ch_ref, cl_ref):
    step = 64

    def some(t, carry):
        rows = pl.ds(pl.multiple_of(t * step, step), step)
        hi, lo = split(c_ref[rows, :])
        ch_ref[rows, :] = hi
        cl_ref[rows, :] = lo
        return carry

    lax.fori_loop(0, c_ref.shape[0] // step, some, 0)


def contract_s(v, c):
    return dot3(v, c)


def arrange_coeffs(c_ref, qh_ref, ql_ref, th_ref, tl_ref, sources):
    rows_dev = c_ref.shape[0] // sources
    for s in range(0, sources, 2):
        for q in range(3):
            block = jnp.concatenate(
                [c_ref[(s + u) * rows_dev + 8 * q : (s + u) * rows_dev + 8 * q + 8, :] for u in range(2)], axis=0
            )
            hi, lo = split(block)
            qh_ref[q, 8 * s : 8 * s + 16, :] = hi
            ql_ref[q, 8 * s : 8 * s + 16, :] = lo
    for s in range(0, sources, 16):
        block = jnp.concatenate(
            [c_ref[(s + u) * rows_dev + 24 : (s + u) * rows_dev + 25, :] for u in range(16)], axis=0
        )
        hi, lo = split(block)
        th_ref[s : s + 16, :] = hi
        tl_ref[s : s + 16, :] = lo


def select(q, local_b):
    shape = (local_b * 64, local_b * LANES)
    row, col = iota(shape, 0), iota(shape, 1)
    sym = sym_index(row & 63)
    lane = GROUP * q + sym if q < 3 else 120 + sym - 5 * ((sym * 52) >> 8)
    return jnp.where(((row >> 6) == (col >> 7)) & ((col & 127) == lane), 1.0, 0.0).astype(BF16)


def unfold(x, q, local_b):
    pick = select(q, local_b)
    return [dot(pick, part, 1, 1).astype(BF16) for part in x]


def contract_r(x, qh_ref, ql_ref, th_ref, tl_ref, local_b):
    total = None
    for q in range(3):
        term = dot3(unfold(x, q, local_b), (qh_ref[q], ql_ref[q]))
        total = term if total is None else total + term
    y = unfold(x, 3, local_b)
    count = y[0].shape[1]
    row, col = iota(y[0].shape, 0), iota(y[0].shape, 1)
    keep = ((sym_index(row & 63) * 52) >> 8) == (col & 7)
    gather = jnp.where((iota((count, count // 8), 0) >> 3) == iota((count, count // 8), 1), 1.0, 0.0).astype(BF16)
    y = [dot(jnp.where(keep, part, jnp.zeros_like(part)), gather).astype(BF16) for part in y]
    return total + dot3(y, (th_ref[...], tl_ref[...]))

VMEM = pl.BlockSpec(memory_space=pltpu.VMEM)
SMEM = pl.BlockSpec(memory_space=pltpu.SMEM)
LIMIT = 60 * 1024 * 1024


def local_kernel(pair_ref, x_ref, c_ref, z_ref, slim_ref, rows_ref, vh_ref, vl_ref, ch_ref, cl_ref):
    kron, last = make_weights(lax.axis_index("pair"), pair_ref, c_ref, slim_ref, rows_ref)
    split_coeffs(c_ref, ch_ref, cl_ref)
    sum_all_pairs(x_ref, kron, last, vh_ref, vl_ref)
    step = 256

    def some(t, carry):
        cols = pl.ds(pl.multiple_of(t * step, step), step)
        z = contract_s((vh_ref[...], vl_ref[...]), (ch_ref[:, cols], cl_ref[:, cols]))
        for j in range(8):
            z_ref[pl.ds(pl.multiple_of(t * step * 8, step * 8) + j, step, stride=8), :] = z[LANES * j : LANES * (j + 1)].T
        return carry

    lax.fori_loop(0, c_ref.shape[1] // step, some, 0)


def local_part(integrals, coeffs, pair_list):
    pairs_dev, rows_dev, basis = integrals.shape
    orbitals = coeffs.shape[1]
    return pl.pallas_call(
        local_kernel,
        out_shape=jax.ShapeDtypeStruct((orbitals * 8, LANES), F32),
        in_specs=[SMEM, VMEM, VMEM],
        out_specs=VMEM,
        scratch_shapes=[
            pltpu.VMEM((basis, LANES), F32),
            pltpu.VMEM((3 * pairs_dev, LANES), F32),
            pltpu.VMEM((8 * LANES, basis), BF16),
            pltpu.VMEM((8 * LANES, basis), BF16),
            pltpu.VMEM((basis, orbitals), BF16),
            pltpu.VMEM((basis, orbitals), BF16),
        ],
        compiler_params=pltpu.CompilerParams(vmem_limit_bytes=LIMIT),
        name="sum_s_and_pairs",
    )(pair_list, integrals.transpose(1, 0, 2), coeffs)


def final_kernel(factor, x_ref, c_ref, o_ref, qh_ref, ql_ref, th_ref, tl_ref):
    sources, local_b = x_ref.shape[:2]
    arrange_coeffs(c_ref, qh_ref, ql_ref, th_ref, tl_ref, sources)
    x = split(jnp.concatenate([x_ref[:, b].reshape(sources * 8, LANES) for b in range(local_b)], axis=1))
    out = factor * contract_r(x, qh_ref, ql_ref, th_ref, tl_ref, local_b)
    o_ref[...] = out.reshape(o_ref.shape)


def final_part(x, coeffs, factor):
    sources, local_b = x.shape[:2]
    orbitals = coeffs.shape[1]
    return pl.pallas_call(
        functools.partial(final_kernel, factor),
        out_shape=jax.ShapeDtypeStruct((local_b, 64, orbitals), F32),
        in_specs=[VMEM, VMEM],
        out_specs=VMEM,
        scratch_shapes=[
            pltpu.VMEM((3, sources * 8, orbitals), BF16),
            pltpu.VMEM((3, sources * 8, orbitals), BF16),
            pltpu.VMEM((sources, orbitals), BF16),
            pltpu.VMEM((sources, orbitals), BF16),
        ],
        compiler_params=pltpu.CompilerParams(vmem_limit_bytes=LIMIT),
        name="sum_r",
    )(x, coeffs)


def body(integrals, coeffs, pair_list):
    basis, orbitals = coeffs.shape
    pair_count, row_count = lax.axis_size("pair"), lax.axis_size("row")
    local_b = orbitals // (pair_count * row_count)
    factor = basis / (2.0 * pair_list.shape[0]) ** 0.5
    z = local_part(integrals, coeffs, pair_list)
    z = lax.psum_scatter(z, "pair", scatter_dimension=0, tiled=True)
    z = z.reshape(row_count, local_b, 8, LANES)
    z = lax.all_to_all(z, "row", split_axis=0, concat_axis=0, tiled=True)
    return final_part(z, coeffs, factor)


def solution(mesh):
    in_specs = (P("pair", "row", None), P(), P())
    out_specs = P(("pair", "row"), None, None)
    return jax.shard_map(body, mesh=mesh, in_specs=in_specs, out_specs=out_specs, check_vma=False)
```

```python
import functools

import jax
import jax.numpy as jnp
from jax import lax
from jax.experimental import pallas as pl
from jax.experimental.pallas import tpu as pltpu
from jax.sharding import PartitionSpec as P

F32, BF16 = jnp.float32, jnp.bfloat16
NACT = 8
STARTS = [8 * i - i * (i - 1) // 2 for i in range(NACT)]
NSYM = 36
GROUP = 40
LANES = 128


def iota(shape, dim):
    return lax.broadcasted_iota(jnp.int32, shape, dim)


def split(x):
    hi = x.astype(BF16)
    return hi, (x - hi.astype(F32)).astype(BF16)


def dot(a, b, ca=1, cb=0, precision=None):
    return lax.dot_general(
        a, b, (((ca,), (cb,)), ((), ())), precision=precision, preferred_element_type=F32
    )


def dot3(a, b, ca=1, cb=0):
    (ah, al), (bh, bl) = a, b
    return dot(ah, bh, ca, cb) + (dot(ah, bl, ca, cb) + dot(al, bh, ca, cb))


def exact(a, b, ca=1, cb=0):
    return dot(a, b, ca, cb, lax.Precision.HIGHEST)


def first_second(m):
    i = jnp.zeros_like(m)
    start = jnp.zeros_like(m)
    for t in range(1, NACT):
        past = (m >= STARTS[t]).astype(jnp.int32)
        i = i + past
        start = start + past * (STARTS[t] - STARTS[t - 1])
    return i, m - start + i


def sym_index(ij):
    i, j = ij >> 3, ij & 7
    low, high = jnp.minimum(i, j), jnp.maximum(i, j)
    return 8 * low - ((low * (low - 1)) >> 1) + high - low


def make_weights(pair, pair_ref, slim_ref, rows_ref):
    pairs_dev = rows_ref.shape[0] // 3

    def pick(n, carry):
        p = pair_ref[pair * pairs_dev + n, 0]
        q = pair_ref[pair * pairs_dev + n, 1]
        rows_ref[pl.ds(n, 1), :] = slim_ref[pl.ds(p, 1), :]
        rows_ref[pl.ds(pairs_dev + n, 1), :] = slim_ref[pl.ds(q, 1), :]
        rows_ref[pl.ds(2 * pairs_dev + n, 1), :] = jnp.full((1, LANES), jnp.where(p != q, 1.0, 0.0), F32)
        return carry

    lax.fori_loop(0, pairs_dev, pick, 0)
    k, m = iota((LANES, LANES), 0), iota((LANES, LANES), 1)
    i, j = first_second(m)
    sel_i = jnp.where((k == i) & (m < NSYM), 1.0, 0.0).astype(F32)
    sel_j = jnp.where((k == j) & (m < NSYM), 1.0, 0.0).astype(F32)
    first, second, distinct = (rows_ref[t * pairs_dev : (t + 1) * pairs_dev, :] for t in range(3))
    weights = exact(first, sel_i) * exact(second, sel_j) + distinct * (
        exact(second, sel_i) * exact(first, sel_j)
    )
    spread = jnp.where(iota((pairs_dev, pairs_dev * 8), 0) == lax.rem(iota((pairs_dev, pairs_dev * 8), 1), pairs_dev), 1.0, 0.0).astype(F32)
    wide = exact(weights, spread, 0, 0)[:GROUP]
    column = lax.div(iota((GROUP, pairs_dev * 8), 1), pairs_dev)
    kron = jnp.concatenate([jnp.where(column == j, wide, 0.0) for j in range(8)], axis=0)
    row, m = iota((64, LANES), 0), iota((64, LANES), 1)
    last = jnp.where(((row & 7) < 5) & (m == 5 * (row >> 3) + (row & 7)), 1.0, 0.0).astype(F32)
    return split(kron), split(exact(last, weights, 1, 1))


def sum_pairs(x_ref, kron, last, vh_ref, vl_ref, s0, width):
    pairs_dev = x_ref.shape[1]
    cols = pl.ds(s0, width)
    parts = [
        dot3(kron, split(x_ref[8 * q : 8 * q + 8, :, cols].reshape(pairs_dev * 8, width))) for q in range(3)
    ]
    tail = dot3(last, split(x_ref[24, :, cols]))
    for j in range(8):
        block = jnp.concatenate(
            [part[GROUP * j : GROUP * (j + 1)] for part in parts] + [tail[8 * j : 8 * j + 8]], axis=0
        )
        hi, lo = split(block)
        vh_ref[LANES * j : LANES * (j + 1), cols] = hi
        vl_ref[LANES * j : LANES * (j + 1), cols] = lo


def split_coeffs(c_ref, ch_ref, cl_ref, start, size):
    rows = pl.ds(start, size)
    hi, lo = split(c_ref[rows, :])
    ch_ref[rows, :] = hi
    cl_ref[rows, :] = lo


def sum_all_pairs(x_ref, kron, last, vh_ref, vl_ref, c_ref, ch_ref, cl_ref):
    basis = x_ref.shape[2]
    step = 256
    whole = basis // step

    def some(t, carry):
        start = pl.multiple_of(t * step, step)
        split_coeffs(c_ref, ch_ref, cl_ref, start, step)
        sum_pairs(x_ref, kron, last, vh_ref, vl_ref, start, step)
        return carry

    lax.fori_loop(0, whole, some, 0)
    if basis % step:
        split_coeffs(c_ref, ch_ref, cl_ref, whole * step, basis % step)
        sum_pairs(x_ref, kron, last, vh_ref, vl_ref, whole * step, basis % step)


def contract_s(v, c):
    return dot3(v, c)


def arrange_coeffs(c_ref, qh_ref, ql_ref, th_ref, tl_ref, sources):
    rows_dev = c_ref.shape[0] // sources
    for s in range(0, sources, 2):
        for q in range(3):
            block = jnp.concatenate(
                [c_ref[(s + u) * rows_dev + 8 * q : (s + u) * rows_dev + 8 * q + 8, :] for u in range(2)], axis=0
            )
            hi, lo = split(block)
            qh_ref[q, 8 * s : 8 * s + 16, :] = hi
            ql_ref[q, 8 * s : 8 * s + 16, :] = lo
    for s in range(0, sources, 16):
        block = jnp.concatenate(
            [c_ref[(s + u) * rows_dev + 24 : (s + u) * rows_dev + 25, :] for u in range(16)], axis=0
        )
        hi, lo = split(block)
        th_ref[s : s + 16, :] = hi
        tl_ref[s : s + 16, :] = lo


def select(q, local_b):
    shape = (local_b * 64, local_b * LANES)
    row, col = iota(shape, 0), iota(shape, 1)
    sym = sym_index(row & 63)
    lane = GROUP * q + sym if q < 3 else 120 + sym - 5 * ((sym * 52) >> 8)
    return jnp.where(((row >> 6) == (col >> 7)) & ((col & 127) == lane), 1.0, 0.0).astype(BF16)


def unfold(x, q, local_b):
    pick = select(q, local_b)
    return [dot(pick, part, 1, 1).astype(BF16) for part in x]


def contract_r(x, qh_ref, ql_ref, th_ref, tl_ref, part, sources, local_b):
    rows = pl.ds(pl.multiple_of(part * (sources * 8), sources * 8), sources * 8)
    total = None
    for q in range(3):
        term = dot3(unfold(x, q, local_b), (qh_ref[q, rows, :], ql_ref[q, rows, :]))
        total = term if total is None else total + term
    y = unfold(x, 3, local_b)
    count = y[0].shape[1]
    row, col = iota(y[0].shape, 0), iota(y[0].shape, 1)
    keep = ((sym_index(row & 63) * 52) >> 8) == (col & 7)
    gather = jnp.where((iota((count, sources), 0) >> 3) == iota((count, sources), 1), 1.0, 0.0).astype(BF16)
    y = [dot(jnp.where(keep, half, jnp.zeros_like(half)), gather).astype(BF16) for half in y]
    rows = pl.ds(pl.multiple_of(part * sources, sources), sources)
    return total + dot3(y, (th_ref[rows, :], tl_ref[rows, :]))

SMEM = pl.BlockSpec(memory_space=pltpu.SMEM)
ANY = pl.BlockSpec(memory_space=pl.ANY)
LIMIT = 62 * 1024 * 1024
MESH = pl.DeviceIdType.MESH
CORES, Y_LO, Y_HI, X, Z = 2, 2, 2, 4, 8
PLANE = X * Z
SIDE = 128
ROWS = SIDE * 8
PIECE = ROWS // X
MESSAGE = ROWS // PLANE


def copy_bytes_of(ref, sem):
    pltpu.make_async_copy(ref, ref, sem).wait()


def kernel(factor, pair_ref, x_hbm, c_hbm, o_ref, x_ref, c_ref, slim_ref, rows_ref, vh_ref, vl_ref, ch_ref, cl_ref,
           qh_ref, ql_ref, th_ref, tl_ref, away_ref, here_ref, core_ref, side_ref, got_ref,
           load_sem, core_send, core_recv, side_send, side_recv, put_send, put_recv):
    pair, row = lax.axis_index("pair"), lax.axis_index("row")
    y_lo, core = pair // CORES, pair % CORES
    y_hi, spot = row // PLANE, row % PLANE
    x = spot // Z
    other_core = (y_lo * CORES + 1 - core, row)
    other_side = ((1 - y_lo) * CORES + core, row)
    corner = (1 - y_lo) * CORES + core, 1 - y_hi

    slim_load = pltpu.make_async_copy(c_hbm.at[:, 0:LANES], slim_ref, load_sem.at[0])
    x_load = pltpu.make_async_copy(x_hbm, x_ref, load_sem.at[1])
    c_load = pltpu.make_async_copy(c_hbm, c_ref, load_sem.at[2])
    slim_load.start()
    x_load.start()
    c_load.start()

    barrier = pltpu.get_barrier_semaphore()
    pl.semaphore_signal(barrier, inc=1, device_id=other_core, device_id_type=MESH)
    pl.semaphore_signal(barrier, inc=1, device_id=other_side, device_id_type=MESH)

    def greet(t, carry):
        pl.semaphore_signal(
            barrier, inc=1, device_id=(corner[0], corner[1] * PLANE + t), device_id_type=MESH
        )
        return carry

    def greet_own(t, carry):
        pl.semaphore_signal(
            barrier, inc=1, device_id=(pair, y_hi * PLANE + (spot + t) % PLANE), device_id_type=MESH
        )
        return carry

    lax.fori_loop(0, PLANE, greet, 0)
    lax.fori_loop(1, PLANE, greet_own, 0)

    slim_load.wait()
    kron, last = make_weights(pair, pair_ref, slim_ref, rows_ref)
    x_load.wait()
    c_load.wait()
    sum_all_pairs(x_ref, kron, last, vh_ref, vl_ref, c_ref, ch_ref, cl_ref)
    pl.semaphore_wait(barrier, 2 * PLANE + 1)

    planes = [(y_lo, 1 - y_hi), (1 - y_lo, y_hi), (1 - y_lo, 1 - y_hi), (y_lo, y_hi)]

    def block(ref, k, start=0, size=ROWS):
        return ref.at[pl.ds(k * ROWS + start, size), :]

    def core_copy(k):
        return pltpu.make_async_remote_copy(
            block(away_ref, k), block(core_ref, k), core_send.at[k], core_recv.at[k],
            device_id=other_core, device_id_type=MESH)

    def spot_x(i):
        return (x + i) % X

    def side_copy(k, i):
        start = spot_x(i) * PIECE
        return pltpu.make_async_remote_copy(
            block(here_ref, k, start, PIECE), block(side_ref, k, start, PIECE), side_send.at[k, i], side_recv.at[k, i],
            device_id=other_side, device_id_type=MESH)

    def compute(k):
        y_lo_to, y_hi_to = planes[k]
        away = (y_lo_to * CORES + 1 - core) * Y_HI + y_hi_to
        here = (y_lo_to * CORES + core) * Y_HI + y_hi_to
        cols = [pl.ds(pl.multiple_of(side * SIDE, SIDE), SIDE) for side in (away, here)]
        c = [jnp.concatenate([ref[:, col] for col in cols], axis=1) for ref in (ch_ref, cl_ref)]
        z = contract_s((vh_ref[...], vl_ref[...]), c)
        for j in range(8):
            part = z[LANES * j : LANES * (j + 1)].T
            away_ref[pl.ds(k * ROWS + j, SIDE, stride=8), :] = part[:SIDE]
            here_ref[pl.ds(k * ROWS + j, SIDE, stride=8), :] = part[SIDE:]
        core_copy(k).start()

    def add_core(k):
        core_copy(k).wait_recv()
        here = block(here_ref, k)
        here[...] += block(core_ref, k)[...]

    def to_side(k):
        add_core(k)
        for i in range(X):
            side_copy(k, i).start()

    def put(u, t, copied_to):
        pltpu.make_async_remote_copy(
            block(here_ref, 2 + u, t * MESSAGE, MESSAGE), got_ref.at[row], put_send.at[u], put_recv.at[u],
            device_id=(copied_to[0], copied_to[1] * PLANE + t), device_id_type=MESH).start()

    def spread(u, copied_to):
        for i in range(X):
            side_copy(u, i).wait_recv()
            start = spot_x(i) * PIECE
            here = block(here_ref, 2 + u, start, PIECE)
            here[...] += block(side_ref, u, start, PIECE)[...]
            own = u == 1 and i == 0

            def one(t, carry):
                put(u, spot_x(i) * Z + (spot + t) % Z, copied_to)
                return carry

            lax.fori_loop(1 if own else 0, Z, one, 0)
            if own:
                pltpu.make_async_copy(
                    block(here_ref, 2 + u, spot * MESSAGE, MESSAGE), got_ref.at[row], put_recv.at[u]).start()

    def take(u, y_hi_from):
        got = got_ref.at[pl.ds(y_hi_from * PLANE, PLANE)]
        copy_bytes_of(got, put_recv.at[u])
        local_b = MESSAGE // 8
        blocks = split(jnp.concatenate([got[:, 8 * b : 8 * b + 8, :].reshape(PLANE * 8, LANES) for b in range(local_b)], axis=1))
        return contract_r(blocks, qh_ref, ql_ref, th_ref, tl_ref, y_hi_from, PLANE, local_b)

    compute(0)
    compute(1)
    to_side(0)
    compute(2)
    to_side(1)
    compute(3)
    add_core(2)
    add_core(3)
    spread(0, corner)
    arrange_coeffs(c_ref, qh_ref, ql_ref, th_ref, tl_ref, Y_HI * PLANE)
    spread(1, (pair, y_hi))
    total = take(0, 1 - y_hi)
    o_ref[...] = factor * (total + take(1, y_hi)).reshape(o_ref.shape)

    for k in range(4):
        core_copy(k).wait_send()
    for k in range(2):
        for i in range(X):
            side_copy(k, i).wait_send()
    copy_bytes_of(block(here_ref, 2), put_send.at[0])
    copy_bytes_of(block(here_ref, 3, 0, ROWS - MESSAGE), put_send.at[1])


def body(integrals, coeffs, pair_list):
    pairs_dev, rows_dev, basis = integrals.shape
    orbitals = coeffs.shape[1]
    factor = basis / (2.0 * pair_list.shape[0]) ** 0.5
    sources = Y_HI * PLANE
    return pl.pallas_call(
        functools.partial(kernel, factor),
        out_shape=jax.ShapeDtypeStruct((SIDE // PLANE, NACT * NACT, orbitals), F32),
        in_specs=[SMEM, ANY, ANY],
        out_specs=pl.BlockSpec(memory_space=pltpu.VMEM),
        scratch_shapes=[
            pltpu.VMEM((rows_dev, pairs_dev, basis), F32),
            pltpu.VMEM((basis, orbitals), F32),
            pltpu.VMEM((basis, LANES), F32),
            pltpu.VMEM((3 * pairs_dev, LANES), F32),
            pltpu.VMEM((8 * LANES, basis), BF16),
            pltpu.VMEM((8 * LANES, basis), BF16),
            pltpu.VMEM((basis, orbitals), BF16),
            pltpu.VMEM((basis, orbitals), BF16),
            pltpu.VMEM((3, sources * 8, orbitals), BF16),
            pltpu.VMEM((3, sources * 8, orbitals), BF16),
            pltpu.VMEM((sources, orbitals), BF16),
            pltpu.VMEM((sources, orbitals), BF16),
            pltpu.VMEM((4 * ROWS, LANES), F32),
            pltpu.VMEM((4 * ROWS, LANES), F32),
            pltpu.VMEM((4 * ROWS, LANES), F32),
            pltpu.VMEM((2 * ROWS, LANES), F32),
            pltpu.VMEM((sources, MESSAGE, LANES), F32),
            pltpu.SemaphoreType.DMA((3,)),
            pltpu.SemaphoreType.DMA((4,)),
            pltpu.SemaphoreType.DMA((4,)),
            pltpu.SemaphoreType.DMA((2, X)),
            pltpu.SemaphoreType.DMA((2, X)),
            pltpu.SemaphoreType.DMA((2,)),
            pltpu.SemaphoreType.DMA((2,)),
        ],
        compiler_params=pltpu.CompilerParams(vmem_limit_bytes=LIMIT, collective_id=0, has_side_effects=True),
        cost_estimate=pl.CostEstimate(flops=15_000_000_000, bytes_accessed=14_000_000, transcendentals=0),
        name="transform",
    )(pair_list, integrals.transpose(1, 0, 2), coeffs)


def solution(mesh):
    in_specs = (P("pair", "row", None), P(), P())
    out_specs = P(("pair", "row"), None, None)
    return jax.shard_map(body, mesh=mesh, in_specs=in_specs, out_specs=out_specs, check_vma=False)
```

```python
import functools

import jax
import jax.numpy as jnp
from jax import lax
from jax.experimental import pallas as pl
from jax.experimental.pallas import tpu as pltpu
from jax.sharding import PartitionSpec as P

F32, BF16 = jnp.float32, jnp.bfloat16
NACT = 8
STARTS = [8 * i - i * (i - 1) // 2 for i in range(NACT)]
NSYM = 36
GROUP = 40
LANES = 128
STEP = 256


def iota(shape, dim):
    return lax.broadcasted_iota(jnp.int32, shape, dim)


def split(x):
    hi = x.astype(BF16)
    return hi, (x - hi.astype(F32)).astype(BF16)


def dot(a, b, ca=1, cb=0, precision=None):
    return lax.dot_general(
        a, b, (((ca,), (cb,)), ((), ())), precision=precision, preferred_element_type=F32
    )


def dot3(a, b, ca=1, cb=0):
    (ah, al), (bh, bl) = a, b
    return dot(ah, bh, ca, cb) + (dot(ah, bl, ca, cb) + dot(al, bh, ca, cb))


def exact(a, b, ca=1, cb=0):
    return dot(a, b, ca, cb, lax.Precision.HIGHEST)


def first_second(m):
    i = jnp.zeros_like(m)
    start = jnp.zeros_like(m)
    for t in range(1, NACT):
        past = (m >= STARTS[t]).astype(jnp.int32)
        i = i + past
        start = start + past * (STARTS[t] - STARTS[t - 1])
    return i, m - start + i


def sym_index(ij):
    i, j = ij >> 3, ij & 7
    low, high = jnp.minimum(i, j), jnp.maximum(i, j)
    return 8 * low - ((low * (low - 1)) >> 1) + high - low


def make_weights(pair, pair_ref, slim_ref, rows_ref):
    pairs_dev = rows_ref.shape[0] // 3

    def pick(n, carry):
        p = pair_ref[0, pair * pairs_dev + n]
        q = pair_ref[1, pair * pairs_dev + n]
        rows_ref[pl.ds(n, 1), :] = slim_ref[pl.ds(p, 1), :]
        rows_ref[pl.ds(pairs_dev + n, 1), :] = slim_ref[pl.ds(q, 1), :]
        rows_ref[pl.ds(2 * pairs_dev + n, 1), :] = jnp.full((1, LANES), jnp.where(p != q, 1.0, 0.0), F32)
        return carry

    lax.fori_loop(0, pairs_dev, pick, 0)
    k, m = iota((LANES, LANES), 0), iota((LANES, LANES), 1)
    i, j = first_second(m)
    sel_i = jnp.where((k == i) & (m < NSYM), 1.0, 0.0).astype(F32)
    sel_j = jnp.where((k == j) & (m < NSYM), 1.0, 0.0).astype(F32)
    first, second, distinct = (rows_ref[t * pairs_dev : (t + 1) * pairs_dev, :] for t in range(3))
    weights = exact(first, sel_i) * exact(second, sel_j) + distinct * (
        exact(second, sel_i) * exact(first, sel_j)
    )
    spread = jnp.where(iota((pairs_dev, pairs_dev * 8), 0) == lax.rem(iota((pairs_dev, pairs_dev * 8), 1), pairs_dev), 1.0, 0.0).astype(F32)
    wide = exact(weights, spread, 0, 0)[:GROUP]
    column = lax.div(iota((GROUP, pairs_dev * 8), 1), pairs_dev)
    kron = jnp.concatenate([jnp.where(column == j, wide, 0.0) for j in range(8)], axis=0)
    row, m = iota((64, LANES), 0), iota((64, LANES), 1)
    last = jnp.where(((row & 7) < 5) & (m == 5 * (row >> 3) + (row & 7)), 1.0, 0.0).astype(F32)
    return split(kron), split(exact(last, weights, 1, 1))


def sum_pairs(x_ref, kron, last, vh_ref, vl_ref, s0, width):
    pairs_dev = x_ref.shape[1]
    cols = pl.ds(s0, width)
    parts = [
        dot3(kron, split(x_ref[8 * q : 8 * q + 8, :, cols].reshape(pairs_dev * 8, width))) for q in range(3)
    ]
    tail = dot3(last, split(x_ref[24, :, cols]))
    for j in range(8):
        block = jnp.concatenate(
            [part[GROUP * j : GROUP * (j + 1)] for part in parts] + [tail[8 * j : 8 * j + 8]], axis=0
        )
        hi, lo = split(block)
        vh_ref[LANES * j : LANES * (j + 1), cols] = hi
        vl_ref[LANES * j : LANES * (j + 1), cols] = lo


def split_coeffs(c_ref, ch_ref, cl_ref, start, size):
    rows = pl.ds(start, size)
    hi, lo = split(c_ref[rows, :])
    ch_ref[rows, :] = hi
    cl_ref[rows, :] = lo


def load_steps(basis):
    return [(start, min(STEP, basis - start)) for start in range(0, basis, STEP)]


def contract_s(v, c):
    return dot3(v, c)


def arrange_coeffs(c_ref, qh_ref, ql_ref, th_ref, tl_ref, sources):
    rows_dev = c_ref.shape[0] // sources
    for s in range(0, sources, 2):
        for q in range(3):
            block = jnp.concatenate(
                [c_ref[(s + u) * rows_dev + 8 * q : (s + u) * rows_dev + 8 * q + 8, :] for u in range(2)], axis=0
            )
            hi, lo = split(block)
            qh_ref[q, 8 * s : 8 * s + 16, :] = hi
            ql_ref[q, 8 * s : 8 * s + 16, :] = lo
    for s in range(0, sources, 16):
        block = jnp.concatenate(
            [c_ref[(s + u) * rows_dev + 24 : (s + u) * rows_dev + 25, :] for u in range(16)], axis=0
        )
        hi, lo = split(block)
        th_ref[s : s + 16, :] = hi
        tl_ref[s : s + 16, :] = lo


def select(q, local_b):
    shape = (local_b * 64, local_b * LANES)
    row, col = iota(shape, 0), iota(shape, 1)
    sym = sym_index(row & 63)
    lane = GROUP * q + sym if q < 3 else 120 + sym - 5 * ((sym * 52) >> 8)
    return jnp.where(((row >> 6) == (col >> 7)) & ((col & 127) == lane), 1.0, 0.0).astype(BF16)


def unfold(x, q, local_b):
    pick = select(q, local_b)
    return [dot(pick, part, 1, 1).astype(BF16) for part in x]


def contract_r(x, qh_ref, ql_ref, th_ref, tl_ref, part, sources, local_b):
    rows = pl.ds(pl.multiple_of(part * (sources * 8), sources * 8), sources * 8)
    total = None
    for q in range(3):
        term = dot3(unfold(x, q, local_b), (qh_ref[q, rows, :], ql_ref[q, rows, :]))
        total = term if total is None else total + term
    y = unfold(x, 3, local_b)
    count = y[0].shape[1]
    row, col = iota(y[0].shape, 0), iota(y[0].shape, 1)
    keep = ((sym_index(row & 63) * 52) >> 8) == (col & 7)
    gather = jnp.where((iota((count, sources), 0) >> 3) == iota((count, sources), 1), 1.0, 0.0).astype(BF16)
    y = [dot(jnp.where(keep, half, jnp.zeros_like(half)), gather).astype(BF16) for half in y]
    rows = pl.ds(pl.multiple_of(part * sources, sources), sources)
    return total + dot3(y, (th_ref[rows, :], tl_ref[rows, :]))

SMEM = pl.BlockSpec(memory_space=pltpu.SMEM)
ANY = pl.BlockSpec(memory_space=pl.ANY)
LIMIT = 62 * 1024 * 1024
MESH = pl.DeviceIdType.MESH
CORES, Y_LO, Y_HI, X, Z = 2, 2, 2, 4, 8
PLANE = X * Z
SIDE = 128
ROWS = SIDE * 8
MESSAGE = ROWS // PLANE


def copy_bytes_of(ref, sem):
    pltpu.make_async_copy(ref, ref, sem).wait()


def kernel(factor, pair_ref, x_hbm, c_hbm, o_ref, x_ref, c_ref, slim_ref, rows_ref, vh_ref, vl_ref, ch_ref, cl_ref,
           qh_ref, ql_ref, th_ref, tl_ref, away_ref, here_ref, core_ref, side_ref, put_ref, got_ref, raw_ref,
           load_sem, core_send, core_recv, side_send, side_recv, put_send, put_recv):
    pair, row = lax.axis_index("pair"), lax.axis_index("row")
    y_lo, core = pair // CORES, pair % CORES
    y_hi, spot = row // PLANE, row % PLANE
    x = spot // Z
    other_core = (y_lo * CORES + 1 - core, row)
    other_side = ((1 - y_lo) * CORES + core, row)
    corner = (1 - y_lo) * CORES + core, 1 - y_hi

    slim_load = pltpu.make_async_copy(c_hbm.at[:, 0:LANES], slim_ref, load_sem.at[0])
    steps = load_steps(c_hbm.shape[0])

    def loads(t, start, size):
        part = pl.ds(start, size)
        return (
            pltpu.make_async_copy(x_hbm.at[:, :, part], x_ref.at[:, :, part], load_sem.at[1 + 2 * t]),
            pltpu.make_async_copy(c_hbm.at[part, :], c_ref.at[part, :], load_sem.at[2 + 2 * t]),
        )

    slim_load.start()
    for t, step in enumerate(steps):
        for load in loads(t, *step):
            load.start()

    barrier = pltpu.get_barrier_semaphore()
    pl.semaphore_signal(barrier, inc=1, device_id=other_core, device_id_type=MESH)
    pl.semaphore_signal(barrier, inc=1, device_id=other_side, device_id_type=MESH)

    def greet(t, carry):
        pl.semaphore_signal(
            barrier, inc=1, device_id=(corner[0], corner[1] * PLANE + t), device_id_type=MESH
        )
        return carry

    def greet_own(t, carry):
        pl.semaphore_signal(
            barrier, inc=1, device_id=(pair, y_hi * PLANE + (spot + t) % PLANE), device_id_type=MESH
        )
        return carry

    lax.fori_loop(0, PLANE, greet, 0)
    lax.fori_loop(1, PLANE, greet_own, 0)

    slim_load.wait()
    kron, last = make_weights(pair, pair_ref, slim_ref, rows_ref)

    def sum_step(t, start, size):
        for load in loads(t, start, size):
            load.wait()
        split_coeffs(c_ref, ch_ref, cl_ref, start, size)
        sum_pairs(x_ref, kron, last, vh_ref, vl_ref, start, size)

    def sum_some(t, carry):
        sum_step(t, pl.multiple_of(t * STEP, STEP), STEP)
        return carry

    whole = sum(size == STEP for _, size in steps)
    lax.fori_loop(0, whole, sum_some, 0)
    for t in range(whole, len(steps)):
        sum_step(t, *steps[t])

    planes = [(y_lo, 1 - y_hi), (1 - y_lo, y_hi), (1 - y_lo, 1 - y_hi), (y_lo, y_hi)]

    def core_copy(k):
        return pltpu.make_async_remote_copy(
            away_ref.at[k], core_ref.at[k], core_send.at[k], core_recv.at[k],
            device_id=other_core, device_id_type=MESH)

    def spot_x(i):
        return (x + i) % X

    def piece(ref, k, i):
        return ref.at[k, :, pl.ds(pl.multiple_of(spot_x(i) * (SIDE // X), SIDE // X), SIDE // X), :]

    def side_copy(k, i):
        return pltpu.make_async_remote_copy(
            piece(here_ref, k, i), piece(side_ref, k, i), side_send.at[k, i], side_recv.at[k, i],
            device_id=other_side, device_id_type=MESH)

    def compute(k):
        y_lo_to, y_hi_to = planes[k]
        away = (y_lo_to * CORES + 1 - core) * Y_HI + y_hi_to
        here = (y_lo_to * CORES + core) * Y_HI + y_hi_to
        cols = [pl.ds(pl.multiple_of(side * SIDE, SIDE), SIDE) for side in (away, here)]
        c = [jnp.concatenate([ref[:, col] for col in cols], axis=1) for ref in (ch_ref, cl_ref)]
        for j in range(0, 8 * LANES, 256):
            rows = slice(j, j + 256)
            raw_ref[k // 2, rows, :] = contract_s((vh_ref[rows, :], vl_ref[rows, :]), c)

    def turn(k):
        for j in range(8):
            part = raw_ref[k // 2, LANES * j : LANES * (j + 1), :].T
            away_ref[k, j] = part[:SIDE]
            here_ref[k, j] = part[SIDE:]
        if k == 0:
            pl.semaphore_wait(barrier, 2 * PLANE + 1)
        core_copy(k).start()

    def add_core(k):
        core_copy(k).wait_recv()
        here_ref[k] += core_ref[k]

    def put(u, t, copied_to):
        pltpu.make_async_remote_copy(
            put_ref.at[u, pl.ds(t * MESSAGE, MESSAGE)], got_ref.at[row], put_send.at[u], put_recv.at[u],
            device_id=(copied_to[0], copied_to[1] * PLANE + t), device_id_type=MESH).start()

    def spread(u, i):
        copied_to = corner if u == 0 else (pair, y_hi)
        side_copy(u, i).wait_recv()
        both = piece(here_ref, 2 + u, i)[...] + piece(side_ref, u, i)[...]
        start = pl.multiple_of(spot_x(i) * (ROWS // X), ROWS // X)
        for j in range(8):
            put_ref[u, pl.ds(start + j, SIDE // X, stride=8), :] = both[j]
        own = u == 1 and i == 0

        def one(t, carry):
            put(u, spot_x(i) * Z + (spot + t) % Z, copied_to)
            return carry

        lax.fori_loop(1 if own else 0, Z, one, 0)
        if own:
            pltpu.make_async_copy(
                put_ref.at[u, pl.ds(spot * MESSAGE, MESSAGE)], got_ref.at[row], put_recv.at[u]).start()

    def take(u, y_hi_from):
        got = got_ref.at[pl.ds(y_hi_from * PLANE, PLANE)]
        copy_bytes_of(got, put_recv.at[u])
        local_b = MESSAGE // 8
        blocks = split(jnp.concatenate([got[:, 8 * b : 8 * b + 8, :].reshape(PLANE * 8, LANES) for b in range(local_b)], axis=1))
        return contract_r(blocks, qh_ref, ql_ref, th_ref, tl_ref, y_hi_from, PLANE, local_b)

    def to_side(k):
        add_core(k)
        for i in range(X):
            side_copy(k, i).start()

    compute(0)
    compute(2)
    turn(0)
    to_side(0)
    compute(1)
    turn(2)
    compute(3)
    turn(1)
    add_core(2)
    spread(0, 0)
    to_side(1)
    spread(0, 1)
    turn(3)
    spread(0, 2)
    add_core(3)
    spread(0, 3)
    arrange_coeffs(c_ref, qh_ref, ql_ref, th_ref, tl_ref, Y_HI * PLANE)
    for i in range(X):
        spread(1, i)
    total = take(0, 1 - y_hi)
    o_ref[...] = factor * (total + take(1, y_hi)).reshape(o_ref.shape)

    for k in range(4):
        core_copy(k).wait_send()
    for k in range(2):
        for i in range(X):
            side_copy(k, i).wait_send()
    copy_bytes_of(put_ref.at[0], put_send.at[0])
    copy_bytes_of(put_ref.at[1, pl.ds(0, ROWS - MESSAGE)], put_send.at[1])


def body(integrals, coeffs, pair_list):
    pairs_dev, rows_dev, basis = integrals.shape
    orbitals = coeffs.shape[1]
    factor = basis / (2.0 * pair_list.shape[0]) ** 0.5
    sources = Y_HI * PLANE
    return pl.pallas_call(
        functools.partial(kernel, factor),
        out_shape=jax.ShapeDtypeStruct((SIDE // PLANE, NACT * NACT, orbitals), F32),
        in_specs=[SMEM, ANY, ANY],
        out_specs=pl.BlockSpec(memory_space=pltpu.VMEM),
        scratch_shapes=[
            pltpu.VMEM((rows_dev, pairs_dev, basis), F32),
            pltpu.VMEM((basis, orbitals), F32),
            pltpu.VMEM((basis, LANES), F32),
            pltpu.VMEM((3 * pairs_dev, LANES), F32),
            pltpu.VMEM((8 * LANES, basis), BF16),
            pltpu.VMEM((8 * LANES, basis), BF16),
            pltpu.VMEM((basis, orbitals), BF16),
            pltpu.VMEM((basis, orbitals), BF16),
            pltpu.VMEM((3, sources * 8, orbitals), BF16),
            pltpu.VMEM((3, sources * 8, orbitals), BF16),
            pltpu.VMEM((sources, orbitals), BF16),
            pltpu.VMEM((sources, orbitals), BF16),
            pltpu.VMEM((4, 8, SIDE, LANES), F32),
            pltpu.VMEM((4, 8, SIDE, LANES), F32),
            pltpu.VMEM((4, 8, SIDE, LANES), F32),
            pltpu.VMEM((2, 8, SIDE, LANES), F32),
            pltpu.VMEM((2, ROWS, LANES), F32),
            pltpu.VMEM((sources, MESSAGE, LANES), F32),
            pltpu.VMEM((2, 8 * LANES, 2 * SIDE), F32),
            pltpu.SemaphoreType.DMA((1 + 2 * len(load_steps(basis)),)),
            pltpu.SemaphoreType.DMA((4,)),
            pltpu.SemaphoreType.DMA((4,)),
            pltpu.SemaphoreType.DMA((2, X)),
            pltpu.SemaphoreType.DMA((2, X)),
            pltpu.SemaphoreType.DMA((2,)),
            pltpu.SemaphoreType.DMA((2,)),
        ],
        compiler_params=pltpu.CompilerParams(vmem_limit_bytes=LIMIT, collective_id=0, has_side_effects=True),
        cost_estimate=pl.CostEstimate(flops=15_000_000_000, bytes_accessed=14_000_000, transcendentals=0),
        name="transform",
    )(pair_list.T, integrals.transpose(1, 0, 2), coeffs)


def solution(mesh):
    in_specs = (P("pair", "row", None), P(), P())
    out_specs = P(("pair", "row"), None, None)
    return jax.shard_map(body, mesh=mesh, in_specs=in_specs, out_specs=out_specs, check_vma=False)
```

```python
import functools

import jax
import jax.numpy as jnp
from jax import lax
from jax.experimental import pallas as pl
from jax.experimental.pallas import tpu as pltpu
from jax.sharding import PartitionSpec as P

F32, BF16 = jnp.float32, jnp.bfloat16
NACT = 8
STARTS = [8 * i - i * (i - 1) // 2 for i in range(NACT)]
NSYM = 36
GROUP = 40
LANES = 128
STEP = 256


def iota(shape, dim):
    return lax.broadcasted_iota(jnp.int32, shape, dim)


def split(x):
    hi = x.astype(BF16)
    return hi, (x - hi.astype(F32)).astype(BF16)


def dot(a, b, ca=1, cb=0, precision=None):
    return lax.dot_general(
        a, b, (((ca,), (cb,)), ((), ())), precision=precision, preferred_element_type=F32
    )


def dot3(a, b, ca=1, cb=0):
    (ah, al), (bh, bl) = a, b
    return dot(ah, bh, ca, cb) + (dot(ah, bl, ca, cb) + dot(al, bh, ca, cb))


def exact(a, b, ca=1, cb=0):
    return dot(a, b, ca, cb, lax.Precision.HIGHEST)


def first_second(m):
    i = jnp.zeros_like(m)
    start = jnp.zeros_like(m)
    for t in range(1, NACT):
        past = (m >= STARTS[t]).astype(jnp.int32)
        i = i + past
        start = start + past * (STARTS[t] - STARTS[t - 1])
    return i, m - start + i


def sym_index(ij):
    i, j = ij >> 3, ij & 7
    low, high = jnp.minimum(i, j), jnp.maximum(i, j)
    return 8 * low - ((low * (low - 1)) >> 1) + high - low


def make_weights(pair, pair_ref, slim_ref, rows_ref):
    pairs_dev = rows_ref.shape[0] // 3

    def pick(n, carry):
        p = pair_ref[0, pair * pairs_dev + n]
        q = pair_ref[1, pair * pairs_dev + n]
        rows_ref[pl.ds(n, 1), :] = slim_ref[pl.ds(p, 1), :]
        rows_ref[pl.ds(pairs_dev + n, 1), :] = slim_ref[pl.ds(q, 1), :]
        rows_ref[pl.ds(2 * pairs_dev + n, 1), :] = jnp.full((1, LANES), jnp.where(p != q, 1.0, 0.0), F32)
        return carry

    lax.fori_loop(0, pairs_dev, pick, 0)
    k, m = iota((LANES, LANES), 0), iota((LANES, LANES), 1)
    i, j = first_second(m)
    sel_i = jnp.where((k == i) & (m < NSYM), 1.0, 0.0).astype(F32)
    sel_j = jnp.where((k == j) & (m < NSYM), 1.0, 0.0).astype(F32)
    first, second, distinct = (rows_ref[t * pairs_dev : (t + 1) * pairs_dev, :] for t in range(3))
    weights = exact(first, sel_i) * exact(second, sel_j) + distinct * (
        exact(second, sel_i) * exact(first, sel_j)
    )
    spread = jnp.where(iota((pairs_dev, pairs_dev * 8), 0) == lax.rem(iota((pairs_dev, pairs_dev * 8), 1), pairs_dev), 1.0, 0.0).astype(F32)
    wide = exact(weights, spread, 0, 0)[:GROUP]
    column = lax.div(iota((GROUP, pairs_dev * 8), 1), pairs_dev)
    kron = jnp.concatenate([jnp.where(column == j, wide, 0.0) for j in range(8)], axis=0)
    row, m = iota((64, LANES), 0), iota((64, LANES), 1)
    last = jnp.where(((row & 7) < 5) & (m == 5 * (row >> 3) + (row & 7)), 1.0, 0.0).astype(F32)
    return split(kron), split(exact(last, weights, 1, 1))


def sum_pairs(x_ref, kron, last, vh_ref, vl_ref, s0, width):
    pairs_dev = x_ref.shape[1]
    cols = pl.ds(s0, width)
    parts = [
        dot3(kron, split(x_ref[8 * q : 8 * q + 8, :, cols].reshape(pairs_dev * 8, width))) for q in range(3)
    ]
    tail = dot3(last, split(x_ref[24, :, cols]))
    for j in range(8):
        block = jnp.concatenate(
            [part[GROUP * j : GROUP * (j + 1)] for part in parts] + [tail[8 * j : 8 * j + 8]], axis=0
        )
        hi, lo = split(block)
        vh_ref[LANES * j : LANES * (j + 1), cols] = hi
        vl_ref[LANES * j : LANES * (j + 1), cols] = lo


def split_coeffs(c_ref, ch_ref, cl_ref, start, size):
    rows = pl.ds(start, size)
    hi, lo = split(c_ref[rows, :])
    ch_ref[rows, :] = hi
    cl_ref[rows, :] = lo


def load_steps(basis):
    return [(start, min(STEP, basis - start)) for start in range(0, basis, STEP)]


def contract_s(v, c):
    return dot3(v, c)


def arrange_coeffs(c_ref, qh_ref, ql_ref, th_ref, tl_ref, sources):
    rows_dev = c_ref.shape[0] // sources
    for s in range(0, sources, 2):
        for q in range(3):
            block = jnp.concatenate(
                [c_ref[(s + u) * rows_dev + 8 * q : (s + u) * rows_dev + 8 * q + 8, :] for u in range(2)], axis=0
            )
            hi, lo = split(block)
            qh_ref[q, 8 * s : 8 * s + 16, :] = hi
            ql_ref[q, 8 * s : 8 * s + 16, :] = lo
    for s in range(0, sources, 16):
        block = jnp.concatenate(
            [c_ref[(s + u) * rows_dev + 24 : (s + u) * rows_dev + 25, :] for u in range(16)], axis=0
        )
        hi, lo = split(block)
        th_ref[s : s + 16, :] = hi
        tl_ref[s : s + 16, :] = lo


def select(q, local_b):
    shape = (local_b * 64, local_b * LANES)
    row, col = iota(shape, 0), iota(shape, 1)
    sym = sym_index(row & 63)
    lane = GROUP * q + sym if q < 3 else 120 + sym - 5 * ((sym * 52) >> 8)
    return jnp.where(((row >> 6) == (col >> 7)) & ((col & 127) == lane), 1.0, 0.0).astype(BF16)


def unfold(x, q, local_b):
    pick = select(q, local_b)
    return [dot(pick, part, 1, 1).astype(BF16) for part in x]


def contract_r(x, qh_ref, ql_ref, th_ref, tl_ref, part, sources, local_b):
    rows = pl.ds(pl.multiple_of(part * (sources * 8), sources * 8), sources * 8)
    total = None
    for q in range(3):
        term = dot3(unfold(x, q, local_b), (qh_ref[q, rows, :], ql_ref[q, rows, :]))
        total = term if total is None else total + term
    y = unfold(x, 3, local_b)
    count = y[0].shape[1]
    row, col = iota(y[0].shape, 0), iota(y[0].shape, 1)
    keep = ((sym_index(row & 63) * 52) >> 8) == (col & 7)
    gather = jnp.where((iota((count, sources), 0) >> 3) == iota((count, sources), 1), 1.0, 0.0).astype(BF16)
    y = [dot(jnp.where(keep, half, jnp.zeros_like(half)), gather).astype(BF16) for half in y]
    rows = pl.ds(pl.multiple_of(part * sources, sources), sources)
    return total + dot3(y, (th_ref[rows, :], tl_ref[rows, :]))

SMEM = pl.BlockSpec(memory_space=pltpu.SMEM)
ANY = pl.BlockSpec(memory_space=pl.ANY)
LIMIT = 62 * 1024 * 1024
MESH = pl.DeviceIdType.MESH
CORES, Y_LO, Y_HI, X, Z = 2, 2, 2, 4, 8
PLANE = X * Z
SIDE = 128
ROWS = SIDE * 8
MESSAGE = ROWS // PLANE


def copy_bytes_of(ref, sem):
    pltpu.make_async_copy(ref, ref, sem).wait()


def kernel(factor, pair_ref, x_hbm, c_hbm, o_ref, x_ref, c_ref, slim_ref, rows_ref, vh_ref, vl_ref, ch_ref, cl_ref,
           qh_ref, ql_ref, th_ref, tl_ref, away_ref, here_ref, core_ref, side_ref, put_ref, got_ref,
           load_sem, core_send, core_recv, side_send, side_recv, put_send, put_recv):
    pair, row = lax.axis_index("pair"), lax.axis_index("row")
    y_lo, core = pair // CORES, pair % CORES
    y_hi, spot = row // PLANE, row % PLANE
    x = spot // Z
    other_core = (y_lo * CORES + 1 - core, row)
    other_side = ((1 - y_lo) * CORES + core, row)
    corner = (1 - y_lo) * CORES + core, 1 - y_hi

    slim_load = pltpu.make_async_copy(c_hbm.at[:, 0:LANES], slim_ref, load_sem.at[0])
    steps = load_steps(c_hbm.shape[0])

    def loads(t, start, size):
        part = pl.ds(start, size)
        return (
            pltpu.make_async_copy(x_hbm.at[:, :, part], x_ref.at[:, :, part], load_sem.at[1 + 2 * t]),
            pltpu.make_async_copy(c_hbm.at[part, :], c_ref.at[part, :], load_sem.at[2 + 2 * t]),
        )

    slim_load.start()
    for t, step in enumerate(steps):
        for load in loads(t, *step):
            load.start()

    barrier = pltpu.get_barrier_semaphore()
    pl.semaphore_signal(barrier, inc=1, device_id=other_core, device_id_type=MESH)
    pl.semaphore_signal(barrier, inc=1, device_id=other_side, device_id_type=MESH)

    def greet(t, carry):
        pl.semaphore_signal(
            barrier, inc=1, device_id=(corner[0], corner[1] * PLANE + t), device_id_type=MESH
        )
        return carry

    def greet_own(t, carry):
        pl.semaphore_signal(
            barrier, inc=1, device_id=(pair, y_hi * PLANE + (spot + t) % PLANE), device_id_type=MESH
        )
        return carry

    lax.fori_loop(0, PLANE, greet, 0)
    lax.fori_loop(1, PLANE, greet_own, 0)

    slim_load.wait()
    kron, last = make_weights(pair, pair_ref, slim_ref, rows_ref)

    def sum_step(t, start, size):
        for load in loads(t, start, size):
            load.wait()
        split_coeffs(c_ref, ch_ref, cl_ref, start, size)
        sum_pairs(x_ref, kron, last, vh_ref, vl_ref, start, size)

    def sum_some(t, carry):
        sum_step(t, pl.multiple_of(t * STEP, STEP), STEP)
        return carry

    whole = sum(size == STEP for _, size in steps)
    lax.fori_loop(0, whole, sum_some, 0)
    for t in range(whole, len(steps)):
        sum_step(t, *steps[t])

    planes = [(y_lo, 1 - y_hi), (1 - y_lo, y_hi), (1 - y_lo, 1 - y_hi), (y_lo, y_hi)]

    def core_copy(k):
        return pltpu.make_async_remote_copy(
            away_ref.at[k], core_ref.at[k], core_send.at[k], core_recv.at[k],
            device_id=other_core, device_id_type=MESH)

    def spot_x(i):
        return (x + i) % X

    def piece(ref, k, i):
        return ref.at[k, :, pl.ds(pl.multiple_of(spot_x(i) * (SIDE // X), SIDE // X), SIDE // X), :]

    def side_copy(k, i):
        return pltpu.make_async_remote_copy(
            piece(here_ref, k, i), piece(side_ref, k, i), side_send.at[k, i], side_recv.at[k, i],
            device_id=other_side, device_id_type=MESH)

    def compute(k):
        y_lo_to, y_hi_to = planes[k]
        away = (y_lo_to * CORES + 1 - core) * Y_HI + y_hi_to
        here = (y_lo_to * CORES + core) * Y_HI + y_hi_to
        cols = [pl.ds(pl.multiple_of(side * SIDE, SIDE), SIDE) for side in (away, here)]
        c = [jnp.concatenate([ref[:, col] for col in cols], axis=1) for ref in (ch_ref, cl_ref)]
        ready = None
        for start in range(0, 8 * LANES + 256, 256):
            done = ready
            if start < 8 * LANES:
                rows = slice(start, start + 256)
                ready = start, contract_s((vh_ref[rows, :], vl_ref[rows, :]), c)
            if done is not None:
                for part in range(0, 256, LANES):
                    turned = done[1][part : part + LANES].T
                    away_ref[k, (done[0] + part) // LANES] = turned[:SIDE]
                    here_ref[k, (done[0] + part) // LANES] = turned[SIDE:]
        if k == 0:
            pl.semaphore_wait(barrier, 2 * PLANE + 1)
        core_copy(k).start()

    def add_core(k):
        core_copy(k).wait_recv()
        here_ref[k] += core_ref[k]

    def put(u, t, copied_to):
        pltpu.make_async_remote_copy(
            put_ref.at[u, pl.ds(t * MESSAGE, MESSAGE)], got_ref.at[row], put_send.at[u], put_recv.at[u],
            device_id=(copied_to[0], copied_to[1] * PLANE + t), device_id_type=MESH).start()

    def spread(u, i):
        copied_to = corner if u == 0 else (pair, y_hi)
        side_copy(u, i).wait_recv()
        both = piece(here_ref, 2 + u, i)[...] + piece(side_ref, u, i)[...]
        start = pl.multiple_of(spot_x(i) * (ROWS // X), ROWS // X)
        for j in range(8):
            put_ref[u, pl.ds(start + j, SIDE // X, stride=8), :] = both[j]
        own = u == 1 and i == 0

        def one(t, carry):
            put(u, spot_x(i) * Z + (spot + t) % Z, copied_to)
            return carry

        lax.fori_loop(1 if own else 0, Z, one, 0)
        if own:
            pltpu.make_async_copy(
                put_ref.at[u, pl.ds(spot * MESSAGE, MESSAGE)], got_ref.at[row], put_recv.at[u]).start()

    def take(u, y_hi_from):
        got = got_ref.at[pl.ds(y_hi_from * PLANE, PLANE)]
        copy_bytes_of(got, put_recv.at[u])
        local_b = MESSAGE // 8
        blocks = split(jnp.concatenate([got[:, 8 * b : 8 * b + 8, :].reshape(PLANE * 8, LANES) for b in range(local_b)], axis=1))
        return contract_r(blocks, qh_ref, ql_ref, th_ref, tl_ref, y_hi_from, PLANE, local_b)

    def to_side(k):
        add_core(k)
        for i in range(X):
            side_copy(k, i).start()

    compute(0)
    to_side(0)
    compute(2)
    compute(1)
    add_core(2)
    spread(0, 0)
    to_side(1)
    spread(0, 1)
    compute(3)
    spread(0, 2)
    add_core(3)
    spread(0, 3)
    arrange_coeffs(c_ref, qh_ref, ql_ref, th_ref, tl_ref, Y_HI * PLANE)
    for i in range(X):
        spread(1, i)
    total = take(0, 1 - y_hi)
    o_ref[...] = factor * (total + take(1, y_hi)).reshape(o_ref.shape)

    for k in range(4):
        core_copy(k).wait_send()
    for k in range(2):
        for i in range(X):
            side_copy(k, i).wait_send()
    copy_bytes_of(put_ref.at[0], put_send.at[0])
    copy_bytes_of(put_ref.at[1, pl.ds(0, ROWS - MESSAGE)], put_send.at[1])


def body(integrals, coeffs, pair_list):
    pairs_dev, rows_dev, basis = integrals.shape
    orbitals = coeffs.shape[1]
    factor = basis / (2.0 * pair_list.shape[0]) ** 0.5
    sources = Y_HI * PLANE
    return pl.pallas_call(
        functools.partial(kernel, factor),
        out_shape=jax.ShapeDtypeStruct((SIDE // PLANE, NACT * NACT, orbitals), F32),
        in_specs=[SMEM, ANY, ANY],
        out_specs=pl.BlockSpec(memory_space=pltpu.VMEM),
        scratch_shapes=[
            pltpu.VMEM((rows_dev, pairs_dev, basis), F32),
            pltpu.VMEM((basis, orbitals), F32),
            pltpu.VMEM((basis, LANES), F32),
            pltpu.VMEM((3 * pairs_dev, LANES), F32),
            pltpu.VMEM((8 * LANES, basis), BF16),
            pltpu.VMEM((8 * LANES, basis), BF16),
            pltpu.VMEM((basis, orbitals), BF16),
            pltpu.VMEM((basis, orbitals), BF16),
            pltpu.VMEM((3, sources * 8, orbitals), BF16),
            pltpu.VMEM((3, sources * 8, orbitals), BF16),
            pltpu.VMEM((sources, orbitals), BF16),
            pltpu.VMEM((sources, orbitals), BF16),
            pltpu.VMEM((4, 8, SIDE, LANES), F32),
            pltpu.VMEM((4, 8, SIDE, LANES), F32),
            pltpu.VMEM((4, 8, SIDE, LANES), F32),
            pltpu.VMEM((2, 8, SIDE, LANES), F32),
            pltpu.VMEM((2, ROWS, LANES), F32),
            pltpu.VMEM((sources, MESSAGE, LANES), F32),
            pltpu.SemaphoreType.DMA((1 + 2 * len(load_steps(basis)),)),
            pltpu.SemaphoreType.DMA((4,)),
            pltpu.SemaphoreType.DMA((4,)),
            pltpu.SemaphoreType.DMA((2, X)),
            pltpu.SemaphoreType.DMA((2, X)),
            pltpu.SemaphoreType.DMA((2,)),
            pltpu.SemaphoreType.DMA((2,)),
        ],
        compiler_params=pltpu.CompilerParams(vmem_limit_bytes=LIMIT, collective_id=0, has_side_effects=True),
        cost_estimate=pl.CostEstimate(flops=15_000_000_000, bytes_accessed=14_000_000, transcendentals=0),
        name="transform",
    )(pair_list.T, integrals.transpose(1, 0, 2), coeffs)


def solution(mesh):
    in_specs = (P("pair", "row", None), P(), P())
    out_specs = P(("pair", "row"), None, None)
    return jax.shard_map(body, mesh=mesh, in_specs=in_specs, out_specs=out_specs, check_vma=False)
```

```python
import functools

import jax
import jax.numpy as jnp
from jax import lax
from jax.experimental import pallas as pl
from jax.experimental.pallas import tpu as pltpu
from jax.sharding import PartitionSpec as P

F32, BF16 = jnp.float32, jnp.bfloat16
NACT = 8
STARTS = [8 * i - i * (i - 1) // 2 for i in range(NACT)]
NSYM = 36
GROUP = 40
LANES = 128
STEP = 256


def iota(shape, dim):
    return lax.broadcasted_iota(jnp.int32, shape, dim)


def split(x):
    hi = x.astype(BF16)
    return hi, (x - hi.astype(F32)).astype(BF16)


def dot(a, b, ca=1, cb=0, precision=None):
    return lax.dot_general(
        a, b, (((ca,), (cb,)), ((), ())), precision=precision, preferred_element_type=F32
    )


def dot3(a, b, ca=1, cb=0):
    (ah, al), (bh, bl) = a, b
    return dot(ah, bh, ca, cb) + (dot(ah, bl, ca, cb) + dot(al, bh, ca, cb))


def exact(a, b, ca=1, cb=0):
    return dot(a, b, ca, cb, lax.Precision.HIGHEST)


def first_second(m):
    i = jnp.zeros_like(m)
    start = jnp.zeros_like(m)
    for t in range(1, NACT):
        past = (m >= STARTS[t]).astype(jnp.int32)
        i = i + past
        start = start + past * (STARTS[t] - STARTS[t - 1])
    return i, m - start + i


def sym_index(ij):
    i, j = ij >> 3, ij & 7
    low, high = jnp.minimum(i, j), jnp.maximum(i, j)
    return 8 * low - ((low * (low - 1)) >> 1) + high - low


def make_weights(pair, pair_ref, slim_ref, rows_ref):
    pairs_dev = rows_ref.shape[0] // 3

    def pick(n, carry):
        p = pair_ref[0, pair * pairs_dev + n]
        q = pair_ref[1, pair * pairs_dev + n]
        rows_ref[pl.ds(n, 1), :] = slim_ref[pl.ds(p, 1), :]
        rows_ref[pl.ds(pairs_dev + n, 1), :] = slim_ref[pl.ds(q, 1), :]
        rows_ref[pl.ds(2 * pairs_dev + n, 1), :] = jnp.full((1, LANES), jnp.where(p != q, 1.0, 0.0), F32)
        return carry

    lax.fori_loop(0, pairs_dev, pick, 0)
    k, m = iota((LANES, LANES), 0), iota((LANES, LANES), 1)
    i, j = first_second(m)
    sel_i = jnp.where((k == i) & (m < NSYM), 1.0, 0.0).astype(F32)
    sel_j = jnp.where((k == j) & (m < NSYM), 1.0, 0.0).astype(F32)
    first, second, distinct = (rows_ref[t * pairs_dev : (t + 1) * pairs_dev, :] for t in range(3))
    weights = exact(first, sel_i) * exact(second, sel_j) + distinct * (
        exact(second, sel_i) * exact(first, sel_j)
    )
    spread = jnp.where(iota((pairs_dev, pairs_dev * 8), 0) == lax.rem(iota((pairs_dev, pairs_dev * 8), 1), pairs_dev), 1.0, 0.0).astype(F32)
    wide = exact(weights, spread, 0, 0)[:GROUP]
    column = lax.div(iota((GROUP, pairs_dev * 8), 1), pairs_dev)
    kron = jnp.concatenate([jnp.where(column == j, wide, 0.0) for j in range(8)], axis=0)
    row, m = iota((64, LANES), 0), iota((64, LANES), 1)
    last = jnp.where(((row & 7) < 5) & (m == 5 * (row >> 3) + (row & 7)), 1.0, 0.0).astype(F32)
    return split(kron), split(exact(last, weights, 1, 1))


def sum_pairs(x_ref, kron, last, vh_ref, vl_ref, s0, width):
    pairs_dev = x_ref.shape[1]
    cols = pl.ds(s0, width)
    parts = [
        dot3(kron, split(x_ref[8 * q : 8 * q + 8, :, cols].reshape(pairs_dev * 8, width))) for q in range(3)
    ]
    tail = dot3(last, split(x_ref[24, :, cols]))
    for j in range(8):
        block = jnp.concatenate(
            [part[GROUP * j : GROUP * (j + 1)] for part in parts] + [tail[8 * j : 8 * j + 8]], axis=0
        )
        hi, lo = split(block)
        vh_ref[LANES * j : LANES * (j + 1), cols] = hi
        vl_ref[LANES * j : LANES * (j + 1), cols] = lo


def split_coeffs(c_ref, ch_ref, cl_ref, start, size):
    rows = pl.ds(start, size)
    hi, lo = split(c_ref[rows, :])
    ch_ref[rows, :] = hi
    cl_ref[rows, :] = lo


def load_steps(basis):
    return [(start, min(STEP, basis - start)) for start in range(0, basis, STEP)]


def contract_s(v, c):
    return dot3(v, c)


def arrange_coeffs(c_ref, qh_ref, ql_ref, th_ref, tl_ref, sources):
    rows_dev = c_ref.shape[0] // sources
    for s in range(0, sources, 2):
        for q in range(3):
            block = jnp.concatenate(
                [c_ref[(s + u) * rows_dev + 8 * q : (s + u) * rows_dev + 8 * q + 8, :] for u in range(2)], axis=0
            )
            hi, lo = split(block)
            qh_ref[q, 8 * s : 8 * s + 16, :] = hi
            ql_ref[q, 8 * s : 8 * s + 16, :] = lo
    for s in range(0, sources, 16):
        block = jnp.concatenate(
            [c_ref[(s + u) * rows_dev + 24 : (s + u) * rows_dev + 25, :] for u in range(16)], axis=0
        )
        hi, lo = split(block)
        th_ref[s : s + 16, :] = hi
        tl_ref[s : s + 16, :] = lo


def select(q, local_b):
    shape = (local_b * 64, local_b * LANES)
    row, col = iota(shape, 0), iota(shape, 1)
    sym = sym_index(row & 63)
    lane = GROUP * q + sym if q < 3 else 120 + sym - 5 * ((sym * 52) >> 8)
    return jnp.where(((row >> 6) == (col >> 7)) & ((col & 127) == lane), 1.0, 0.0).astype(BF16)


def unfold(x, q, local_b):
    pick = select(q, local_b)
    return [dot(pick, part, 1, 1).astype(BF16) for part in x]


def contract_r(x, qh_ref, ql_ref, th_ref, tl_ref, part, sources, local_b):
    rows = pl.ds(pl.multiple_of(part * (sources * 8), sources * 8), sources * 8)
    total = None
    for q in range(3):
        term = dot3(unfold(x, q, local_b), (qh_ref[q, rows, :], ql_ref[q, rows, :]))
        total = term if total is None else total + term
    y = unfold(x, 3, local_b)
    count = y[0].shape[1]
    row, col = iota(y[0].shape, 0), iota(y[0].shape, 1)
    keep = ((sym_index(row & 63) * 52) >> 8) == (col & 7)
    gather = jnp.where((iota((count, sources), 0) >> 3) == iota((count, sources), 1), 1.0, 0.0).astype(BF16)
    y = [dot(jnp.where(keep, half, jnp.zeros_like(half)), gather).astype(BF16) for half in y]
    rows = pl.ds(pl.multiple_of(part * sources, sources), sources)
    return total + dot3(y, (th_ref[rows, :], tl_ref[rows, :]))

SMEM = pl.BlockSpec(memory_space=pltpu.SMEM)
ANY = pl.BlockSpec(memory_space=pl.ANY)
LIMIT = 62 * 1024 * 1024
MESH = pl.DeviceIdType.MESH
CORES, Y_LO, Y_HI, X, Z = 2, 2, 2, 4, 8
PLANE = X * Z
SIDE = 128
ROWS = SIDE * 8
MESSAGE = ROWS // PLANE


def copy_bytes_of(ref, sem):
    pltpu.make_async_copy(ref, ref, sem).wait()


def kernel(factor, pair_ref, x_hbm, c_hbm, o_ref, x_ref, c_ref, slim_ref, rows_ref, vh_ref, vl_ref, ch_ref, cl_ref,
           qh_ref, ql_ref, th_ref, tl_ref, away_ref, here_ref, core_ref, side_ref, put_ref, got_ref,
           load_sem, core_send, core_recv, side_send, side_recv, put_send, put_recv):
    pair, row = lax.axis_index("pair"), lax.axis_index("row")
    y_lo, core = pair // CORES, pair % CORES
    y_hi, spot = row // PLANE, row % PLANE
    x = spot // Z
    other_core = (y_lo * CORES + 1 - core, row)
    other_side = ((1 - y_lo) * CORES + core, row)
    corner = (1 - y_lo) * CORES + core, 1 - y_hi

    barrier = pltpu.get_barrier_semaphore()
    pl.semaphore_signal(barrier, inc=1, device_id=other_core, device_id_type=MESH)
    pl.semaphore_signal(barrier, inc=1, device_id=other_side, device_id_type=MESH)

    def greet(t, carry):
        pl.semaphore_signal(
            barrier, inc=1, device_id=(corner[0], corner[1] * PLANE + t), device_id_type=MESH
        )
        return carry

    def greet_own(t, carry):
        pl.semaphore_signal(
            barrier, inc=1, device_id=(pair, y_hi * PLANE + (spot + t) % PLANE), device_id_type=MESH
        )
        return carry

    lax.fori_loop(0, PLANE, greet, 0)
    lax.fori_loop(1, PLANE, greet_own, 0)

    slim_load = pltpu.make_async_copy(c_hbm.at[:, 0:LANES], slim_ref, load_sem.at[0])
    steps = load_steps(c_hbm.shape[0])

    def loads(t, start, size):
        part = pl.ds(start, size)
        return (
            pltpu.make_async_copy(x_hbm.at[:, :, part], x_ref.at[:, :, part], load_sem.at[1 + 2 * t]),
            pltpu.make_async_copy(c_hbm.at[part, :], c_ref.at[part, :], load_sem.at[2 + 2 * t]),
        )

    slim_load.start()
    for t, step in enumerate(steps):
        for load in loads(t, *step):
            load.start()

    slim_load.wait()
    kron, last = make_weights(pair, pair_ref, slim_ref, rows_ref)

    def sum_step(t, start, size):
        for load in loads(t, start, size):
            load.wait()
        split_coeffs(c_ref, ch_ref, cl_ref, start, size)
        sum_pairs(x_ref, kron, last, vh_ref, vl_ref, start, size)

    def sum_some(t, carry):
        sum_step(t, pl.multiple_of(t * STEP, STEP), STEP)
        return carry

    whole = sum(size == STEP for _, size in steps)
    lax.fori_loop(0, whole, sum_some, 0)
    for t in range(whole, len(steps)):
        sum_step(t, *steps[t])

    planes = [(y_lo, 1 - y_hi), (1 - y_lo, y_hi), (1 - y_lo, 1 - y_hi), (y_lo, y_hi)]

    def core_copy(k):
        return pltpu.make_async_remote_copy(
            away_ref.at[k], core_ref.at[k], core_send.at[k], core_recv.at[k],
            device_id=other_core, device_id_type=MESH)

    def spot_x(i):
        return (x + i) % X

    def piece(ref, k, i):
        return ref.at[k, :, pl.ds(pl.multiple_of(spot_x(i) * (SIDE // X), SIDE // X), SIDE // X), :]

    def side_copy(k, i):
        return pltpu.make_async_remote_copy(
            piece(here_ref, k, i), piece(side_ref, k, i), side_send.at[k, i], side_recv.at[k, i],
            device_id=other_side, device_id_type=MESH)

    def compute(k):
        y_lo_to, y_hi_to = planes[k]
        away = (y_lo_to * CORES + 1 - core) * Y_HI + y_hi_to
        here = (y_lo_to * CORES + core) * Y_HI + y_hi_to
        cols = [pl.ds(pl.multiple_of(side * SIDE, SIDE), SIDE) for side in (away, here)]
        c = [jnp.concatenate([ref[:, col] for col in cols], axis=1) for ref in (ch_ref, cl_ref)]
        ready = None
        for start in range(0, 8 * LANES + 256, 256):
            done = ready
            if start < 8 * LANES:
                rows = slice(start, start + 256)
                ready = start, contract_s((vh_ref[rows, :], vl_ref[rows, :]), c)
            if done is not None:
                for part in range(0, 256, LANES):
                    turned = done[1][part : part + LANES].T
                    away_ref[k, (done[0] + part) // LANES] = turned[:SIDE]
                    here_ref[k, (done[0] + part) // LANES] = turned[SIDE:]
        if k == 0:
            pl.semaphore_wait(barrier, 2 * PLANE + 1)
        core_copy(k).start()

    def add_core(k):
        core_copy(k).wait_recv()
        here_ref[k] += core_ref[k]

    def put(u, t, copied_to):
        pltpu.make_async_remote_copy(
            put_ref.at[u, pl.ds(t * MESSAGE, MESSAGE)], got_ref.at[row], put_send.at[u], put_recv.at[u],
            device_id=(copied_to[0], copied_to[1] * PLANE + t), device_id_type=MESH).start()

    def spread(u, i):
        copied_to = corner if u == 0 else (pair, y_hi)
        side_copy(u, i).wait_recv()
        both = piece(here_ref, 2 + u, i)[...] + piece(side_ref, u, i)[...]
        start = pl.multiple_of(spot_x(i) * (ROWS // X), ROWS // X)
        for j in range(8):
            put_ref[u, pl.ds(start + j, SIDE // X, stride=8), :] = both[j]
        own = u == 1 and i == 0

        def one(t, carry):
            put(u, spot_x(i) * Z + (spot + t) % Z, copied_to)
            return carry

        lax.fori_loop(1 if own else 0, Z, one, 0)
        if own:
            pltpu.make_async_copy(
                put_ref.at[u, pl.ds(spot * MESSAGE, MESSAGE)], got_ref.at[row], put_recv.at[u]).start()

    def take(u, y_hi_from):
        got = got_ref.at[pl.ds(y_hi_from * PLANE, PLANE)]
        copy_bytes_of(got, put_recv.at[u])
        local_b = MESSAGE // 8
        blocks = split(jnp.concatenate([got[:, 8 * b : 8 * b + 8, :].reshape(PLANE * 8, LANES) for b in range(local_b)], axis=1))
        return contract_r(blocks, qh_ref, ql_ref, th_ref, tl_ref, y_hi_from, PLANE, local_b)

    def to_side(k):
        add_core(k)
        for i in range(X):
            side_copy(k, i).start()

    compute(0)
    to_side(0)
    compute(2)
    compute(1)
    add_core(2)
    spread(0, 0)
    to_side(1)
    spread(0, 1)
    compute(3)
    spread(0, 2)
    add_core(3)
    spread(0, 3)
    spread(1, 0)
    arrange_coeffs(c_ref, qh_ref, ql_ref, th_ref, tl_ref, Y_HI * PLANE)
    for i in range(1, X):
        spread(1, i)
    total = take(0, 1 - y_hi)
    o_ref[...] = factor * (total + take(1, y_hi)).reshape(o_ref.shape)

    for k in range(4):
        core_copy(k).wait_send()
    for k in range(2):
        for i in range(X):
            side_copy(k, i).wait_send()
    copy_bytes_of(put_ref.at[0], put_send.at[0])
    copy_bytes_of(put_ref.at[1, pl.ds(0, ROWS - MESSAGE)], put_send.at[1])


def body(integrals, coeffs, pair_list):
    pairs_dev, rows_dev, basis = integrals.shape
    orbitals = coeffs.shape[1]
    factor = basis / (2.0 * pair_list.shape[0]) ** 0.5
    sources = Y_HI * PLANE
    return pl.pallas_call(
        functools.partial(kernel, factor),
        out_shape=jax.ShapeDtypeStruct((SIDE // PLANE, NACT * NACT, orbitals), F32),
        in_specs=[SMEM, ANY, ANY],
        out_specs=pl.BlockSpec(memory_space=pltpu.VMEM),
        scratch_shapes=[
            pltpu.VMEM((rows_dev, pairs_dev, basis), F32),
            pltpu.VMEM((basis, orbitals), F32),
            pltpu.VMEM((basis, LANES), F32),
            pltpu.VMEM((3 * pairs_dev, LANES), F32),
            pltpu.VMEM((8 * LANES, basis), BF16),
            pltpu.VMEM((8 * LANES, basis), BF16),
            pltpu.VMEM((basis, orbitals), BF16),
            pltpu.VMEM((basis, orbitals), BF16),
            pltpu.VMEM((3, sources * 8, orbitals), BF16),
            pltpu.VMEM((3, sources * 8, orbitals), BF16),
            pltpu.VMEM((sources, orbitals), BF16),
            pltpu.VMEM((sources, orbitals), BF16),
            pltpu.VMEM((4, 8, SIDE, LANES), F32),
            pltpu.VMEM((4, 8, SIDE, LANES), F32),
            pltpu.VMEM((4, 8, SIDE, LANES), F32),
            pltpu.VMEM((2, 8, SIDE, LANES), F32),
            pltpu.VMEM((2, ROWS, LANES), F32),
            pltpu.VMEM((sources, MESSAGE, LANES), F32),
            pltpu.SemaphoreType.DMA((1 + 2 * len(load_steps(basis)),)),
            pltpu.SemaphoreType.DMA((4,)),
            pltpu.SemaphoreType.DMA((4,)),
            pltpu.SemaphoreType.DMA((2, X)),
            pltpu.SemaphoreType.DMA((2, X)),
            pltpu.SemaphoreType.DMA((2,)),
            pltpu.SemaphoreType.DMA((2,)),
        ],
        compiler_params=pltpu.CompilerParams(vmem_limit_bytes=LIMIT, collective_id=0, has_side_effects=True),
        cost_estimate=pl.CostEstimate(flops=15_000_000_000, bytes_accessed=14_000_000, transcendentals=0),
        name="transform",
    )(pair_list.T, integrals.transpose(1, 0, 2), coeffs)


def solution(mesh):
    in_specs = (P("pair", "row", None), P(), P())
    out_specs = P(("pair", "row"), None, None)
    return jax.shard_map(body, mesh=mesh, in_specs=in_specs, out_specs=out_specs, check_vma=False)
```
